32 devices in a mesh: groups: 2 (over y), ep: 4 (over x, core), tp: 4 (over z).
Axes of the slice: x: 2, y: 2, z: 4, core: 2. Of those that a mesh axis runs over, the one named last changes fastest.
Arguments:
- hidden_in: bfloat16 [32, 4, 3584], P(('groups', 'ep', 'tp')), parts along dimension 0, may hold values from -12 to 12
- queries: bfloat16 [32, 4, 128, 576], P(('groups', 'ep', 'tp')), parts along dimension 0, may hold values from -100 to 100
- kv_cache: bfloat16 [32, 2048, 576], P(('groups', 'ep', 'tp')), parts along dimension 0, may hold values from -6 to 6
- new_kv: bfloat16 [32, 4, 576], P(('groups', 'ep', 'tp')), parts along dimension 0, may hold values from -8 to 8
- lengths: int32 [32], P(('groups', 'ep', 'tp')), parts along dimension 0, may hold values from 128 to 2048, as said below
- expert_ids: int32 [32, 4, 2], P(('groups', 'ep')), parts along dimension 0, may hold values from 0 to 3, all different within a row; in each aligned block of 16 rows (0 to 15, 16 to 31, ..., all dimensions but the last counted through in order) at most 12 rows name the same one
- value_up: bfloat16 [128, 512, 128], P(('ep', 'tp')), may hold values from -3 to 3
- out_proj: bfloat16 [128, 128, 3584], P(('ep', 'tp')), may hold values from -0.046875 to 0.046875
- norm_gain: bfloat16 [3584], replicated, may hold values from 0.099609375 to 1.8984375
- router: bfloat16 [3584, 4], replicated, may hold values from -0.09375 to 0.09375
- expert_in: bfloat16 [4, 2, 3584, 2048], P('ep', None, None, 'tp'), may hold values from -0.09375 to 0.09375
- expert_out: bfloat16 [4, 2048, 3584], P('ep', 'tp'), may hold values from -0.125 to 0.125
- shared_in: bfloat16 [2, 3584, 1024], P(None, None, 'tp'), may hold values from -0.09375 to 0.09375
- shared_out: bfloat16 [1024, 3584], P('tp'), may hold values from -0.1875 to 0.1875
Outputs:
- layer_out: bfloat16 [32, 4, 3584], P(('groups', 'ep', 'tp')), parts along dimension 0
The draws below stay inside these ranges and needn't reach their ends.
There are 2 independent parts, one for each index of `groups`. The reference program is written for one: setup_inputs(seed, part) draws one part's arguments, and reference() takes and returns one part's arrays. A program takes and returns all parts, laid end to end along the dimension named above; an argument that names none is the same for every part. Nothing has to cross between parts.
Inputs may be any that keep to these rules, and one draw needn't show every extreme that they name: `expert_ids`: each row and step names 2 distinct experts; within the rows of one index of ep, over all 4 steps, no expert is named more than 12 times, and in every draw some expert is named exactly 12 times there. `lengths`: some row uses all 2048 cached positions.
All inputs are finite; a program needn't handle non-finite values.
Results may differ from the reference program's by a relative error of at most 0.014.
Values may be sent and summed in bfloat16 or wider, within the bound.
A program may use at most 64 MiB of HBM per device.

```python
import math
import jax
import jax.numpy as jnp
import numpy as np
from jax import lax

D = 3584
HEADS = 128
LAT = 512
VHEAD = 128
MOE_FF = 2048
SH_FF = 1024
STEPS = 4
CTX = 2048
KV = 576
EXPERTS = 4
TOP = 2
ROWS_EP = 4
ROWS = 16
CAP = 12


def align_draws(key):
    key_fresh = jax.random.fold_in(key, 11)
    key_query = jax.random.fold_in(key, 13)
    fresh = jax.random.normal(key_fresh, (ROWS, STEPS, KV), jnp.float32)
    query_all = 0.5 * jax.random.normal(key_query, (ROWS, STEPS, HEADS, KV), jnp.float32)
    return (fresh, query_all)


def draw_queries(key, part):
    return align_draws(key)[1].astype(jnp.bfloat16)


def draw_new_kv(key, part):
    return align_draws(key)[0].astype(jnp.bfloat16)


def draw_lengths(key, part):
    key_base = jax.random.fold_in(key, 21)
    key_index = jax.random.fold_in(key, 22)
    base = jax.random.randint(key_base, (ROWS,), CTX // 16, CTX + 1, dtype=jnp.int32)
    longest = jax.random.randint(key_index, (), 0, ROWS, dtype=jnp.int32)
    return base.at[longest].set(CTX).astype(jnp.int32)


def draw_hidden_in(key, part):
    key_columns = jax.random.fold_in(key, 31)
    key_base = jax.random.fold_in(key, 32)
    column_scale = jnp.exp(jax.random.uniform(key_columns, (D,), jnp.float32, 0.0, math.log(10.0)))
    column_scale = column_scale / jnp.sqrt(jnp.mean(column_scale * column_scale))
    base = jax.random.normal(key_base, (ROWS, STEPS, D), jnp.float32)
    return (0.5 * base * column_scale).astype(jnp.bfloat16)


def shard_levels(own_key, extent, shards, low, top_value):
    def one(axis_at, blocks):
        heights = jax.random.uniform(jax.random.fold_in(jax.random.fold_in(own_key, 6), axis_at), (blocks,), jnp.float32, low / len(shards), top_value / len(shards))
        return jnp.repeat(jnp.exp(heights), extent[axis_at] // blocks).reshape((-1,) + (1,) * (len(extent) - axis_at - 1))

    factor_of = one(*shards[0])
    for cut in shards[1:]:
        factor_of = factor_of * one(*cut)
    return factor_of


def assign_block(rng, own, number, rows, count, top, reach, lean):
    sequence = jax.random.permutation(rng, count)
    heavy_load, ordinary = shares(count, rows * top, reach, lean, True), shares(count, rows * top, reach, lean, False)
    places = jnp.arange(count)

    def named(sizes, offset_by):
        used = int((sizes > 0).sum())
        fixed = max(1, used // 4)
        shifted = fixed + (places - fixed + offset_by * (used - fixed)) % max(1, count - fixed)
        return jnp.zeros((count,), jnp.int32).at[sequence[jnp.where(places < fixed, places, shifted)]].set(jnp.asarray(sizes, jnp.int32))

    sizes = jnp.where(number % 4 == 0, named(heavy_load, number // 4), named(ordinary, number - number // 4 - 1))
    mixed = jax.random.permutation(jax.random.fold_in(own, 3), count)
    donor, taker = mixed[0:count // 2 * 2:2], mixed[1:count // 2 * 2:2]
    room = jnp.minimum(sizes[donor] - 1, reach - sizes[taker]) // 2
    room = jnp.where((donor == sequence[0]) | (taker == sequence[0]) | (sizes[taker] == 0), 0, jnp.maximum(room, 0))
    shifted = jax.random.randint(jax.random.fold_in(own, 4), (count // 2,), 0, 1 << 20) % (room + 1)
    sizes = sizes.at[donor].add(-shifted).at[taker].add(shifted)
    items = jnp.searchsorted(jnp.cumsum(sizes), jnp.arange(rows * top), side="right").astype(jnp.int32)
    table = items.reshape(top, rows).T
    table = table[jax.random.permutation(jax.random.fold_in(own, 1), rows)]
    offset_by = jax.random.randint(jax.random.fold_in(own, 2), (rows, 1), 0, top)
    return jnp.take_along_axis(table, (jnp.arange(top)[None, :] + offset_by) % top, axis=1)


def shares(amount, total, most, skew, full):
    portions = [(1 << 20) // math.isqrt(rank ** skew) + 1 for rank in range(1, amount + 1)]
    largest = most if full else min(most, max(-(-total // amount), total * portions[0] // sum(portions)))
    least = 1 if total - largest >= amount - 1 else 0
    holding, rest = [largest] + [least] * (amount - 1), total - largest - least * (amount - 1)
    while rest > 0:
        movable = [i for i in range(1, amount) if holding[i] < largest] or [i for i in range(1, amount) if holding[i] < most]
        mass, left = sum([portions[i] for i in movable]), rest
        for i in movable:
            extra = min(most - holding[i], max(1, left * portions[i] // mass), rest)
            holding[i] = holding[i] + extra
            rest = rest - extra
    return np.array(holding)


def gaussian(key, dims, spread, bound, split=(), kind=jnp.bfloat16):
    entries = jax.random.normal(key, dims, jnp.float32) * spread
    if len(split) > 0:
        entries = shard_levels(key, dims, split, -0.22, 0.18) * entries
    return jnp.clip(entries, min=-bound, max=bound).astype(kind)


def setup_inputs(seed: int = 0, part: int = 0) -> dict:
    streams_of = jax.random.split(jax.random.key(seed), 15)
    part_keys = jax.random.split(jax.random.fold_in(streams_of[14], part), 15)
    hidden_in = draw_hidden_in(jax.random.fold_in(jax.random.fold_in(streams_of[14], part), 71), part)
    queries = draw_queries(jax.random.fold_in(jax.random.fold_in(streams_of[14], part), 71), part)
    kv_cache = gaussian(part_keys[2], (ROWS, CTX, KV), 1.0, 6.0, ((0, 16),))
    new_kv = draw_new_kv(jax.random.fold_in(jax.random.fold_in(streams_of[14], part), 71), part)
    lengths = draw_lengths(jax.random.fold_in(jax.random.fold_in(streams_of[14], part), 71), part)
    expert_ids_keys = jax.random.split(jax.random.fold_in(part_keys[5], 1), ROWS * STEPS // (ROWS_EP * STEPS))
    expert_ids_turns = jax.random.permutation(jax.random.fold_in(part_keys[5], 3), ROWS * STEPS // (ROWS_EP * STEPS))
    expert_ids = jax.vmap(lambda own, number: assign_block(jax.random.fold_in(part_keys[5], 2), own, number, ROWS_EP * STEPS, EXPERTS, TOP, CAP, 3))(expert_ids_keys, expert_ids_turns).reshape((ROWS, STEPS, TOP))
    value_up = gaussian(streams_of[6], (HEADS, LAT, VHEAD), (max(LAT // 128, 1)) ** -0.5, 3.0, ((0, 16),))
    out_proj = gaussian(streams_of[7], (HEADS, VHEAD, D), (HEADS * VHEAD) ** -0.5, 0.046875, ((0, 16),))
    norm_gain = jnp.clip(1.0 + 0.18 * jax.random.normal(streams_of[8], (D,), jnp.float32), 0.099609375, 1.8984375).astype(jnp.bfloat16)
    router = gaussian(streams_of[9], (D, EXPERTS), D ** -0.5, 0.09375)
    expert_in = gaussian(streams_of[10], (EXPERTS, 2, D, MOE_FF), D ** -0.5, 0.09375, ((0, 4), (3, 4)))
    expert_out = gaussian(streams_of[11], (EXPERTS, MOE_FF, D), MOE_FF ** -0.5, 0.125, ((0, 4), (1, 4)))
    shared_in = gaussian(streams_of[12], (2, D, SH_FF), D ** -0.5, 0.09375, ((2, 4),))
    shared_out = gaussian(streams_of[13], (SH_FF, D), SH_FF ** -0.5, 0.1875, ((0, 4),))
    return {"hidden_in": hidden_in, "queries": queries, "kv_cache": kv_cache, "new_kv": new_kv, "lengths": lengths, "expert_ids": expert_ids, "value_up": value_up, "out_proj": out_proj, "norm_gain": norm_gain, "router": router, "expert_in": expert_in, "expert_out": expert_out, "shared_in": shared_in, "shared_out": shared_out}


score_scale = 192.0 ** (-0.5)
route_scale = 2.5
norm_eps = 1e-06

def attend_row(operands):
    query_row, cache_row, recent_row, length_row = operands
    steps_here, heads_here, kv_width = query_row.shape
    positions = cache_row.shape[0]
    flattened = query_row.reshape(steps_here * heads_here, kv_width)
    cached = jnp.dot(flattened, cache_row.T, preferred_element_type=jnp.float32).reshape(steps_here, heads_here, positions) * score_scale
    recent = jnp.dot(flattened, recent_row.T, preferred_element_type=jnp.float32).reshape(steps_here, heads_here, steps_here) * score_scale
    cache_live = jnp.arange(positions, dtype=jnp.int32) < length_row
    causal = jnp.arange(steps_here, dtype=jnp.int32)[None, :] <= jnp.arange(steps_here, dtype=jnp.int32)[:, None]
    cached = jnp.where(cache_live[None, None, :], cached, -1e+30)
    recent = jnp.where(causal[:, None, :], recent, -1e+30)
    highest = jnp.maximum(cached.max(-1), recent.max(-1))[..., None]
    cached_exp = jnp.exp(cached - highest)
    recent_exp = jnp.exp(recent - highest)
    denominator = cached_exp.sum(-1, keepdims=True) + recent_exp.sum(-1, keepdims=True)
    cached_prob = (cached_exp / denominator).astype(jnp.bfloat16)
    recent_prob = (recent_exp / denominator).astype(jnp.bfloat16)
    combined = jnp.dot(cached_prob.reshape(steps_here * heads_here, positions), cache_row, preferred_element_type=jnp.float32)
    combined = combined + jnp.dot(recent_prob.reshape(steps_here * heads_here, steps_here), recent_row, preferred_element_type=jnp.float32)
    return combined.reshape(steps_here, heads_here, kv_width)[:, :, :LAT].astype(jnp.bfloat16)

def head_values(operands):
    head_latent, head_weight = operands
    return jnp.dot(head_latent, head_weight, preferred_element_type=jnp.float32).astype(jnp.bfloat16)

def reference(hidden_in, queries, kv_cache, new_kv, lengths, expert_ids, value_up, out_proj, norm_gain, router, expert_in, expert_out, shared_in, shared_out):
    latent_out = lax.map(attend_row, (queries, kv_cache, new_kv, lengths))
    latent_heads = jnp.transpose(latent_out, (2, 0, 1, 3)).reshape(HEADS, ROWS * STEPS, LAT)
    values = lax.map(head_values, (latent_heads, value_up))
    flat_values = jnp.transpose(values, (1, 0, 2)).reshape(ROWS * STEPS, HEADS * VHEAD)
    attention = jnp.dot(flat_values, out_proj.reshape(HEADS * VHEAD, D), preferred_element_type=jnp.float32)
    residual = hidden_in.astype(jnp.float32).reshape(ROWS * STEPS, D) + attention
    mean_square = lax.optimization_barrier(jnp.mean(residual * residual, axis=-1, keepdims=True))
    item_rows = (residual * lax.rsqrt(mean_square + norm_eps) * norm_gain.astype(jnp.float32)).astype(jnp.bfloat16)
    affinity = jax.nn.sigmoid(jnp.dot(item_rows, router, preferred_element_type=jnp.float32))
    picked = expert_ids.reshape(ROWS * STEPS, TOP)
    chosen = lax.optimization_barrier(jnp.sum((picked[:, :, None] == jnp.arange(EXPERTS, dtype=jnp.int32)[None, None, :]).astype(jnp.float32), axis=1))
    scored = chosen * affinity
    gate_weight = route_scale * scored / lax.optimization_barrier(jnp.sum(scored, axis=-1, keepdims=True))

    def add_expert(running, operands):
        weight_in, weight_out, item_share = operands
        gate_part = jnp.dot(item_rows, weight_in[0], preferred_element_type=jnp.float32)
        up_part = jnp.dot(item_rows, weight_in[1], preferred_element_type=jnp.float32)
        activated = (jax.nn.silu(gate_part) * up_part).astype(jnp.bfloat16)
        produced = jnp.dot(activated, weight_out, preferred_element_type=jnp.float32)
        return (running + item_share[:, None] * produced, None)
    routed, unused = lax.scan(add_expert, jnp.zeros((ROWS * STEPS, D), jnp.float32), (expert_in, expert_out, gate_weight.T))
    shared_gate = jnp.dot(item_rows, shared_in[0], preferred_element_type=jnp.float32)
    shared_up = jnp.dot(item_rows, shared_in[1], preferred_element_type=jnp.float32)
    shared_act = (jax.nn.silu(shared_gate) * shared_up).astype(jnp.bfloat16)
    shared = jnp.dot(shared_act, shared_out, preferred_element_type=jnp.float32)
    layer_out = (residual + routed + shared).astype(jnp.bfloat16)
    return layer_out.reshape(ROWS, STEPS, D)
```

```python
import functools

import jax
import jax.numpy as jnp
from jax import lax
from jax.experimental import pallas as pl
from jax.experimental.pallas import tpu as pltpu
from jax.sharding import PartitionSpec as P

score_scale = 192.0 ** (-0.5)
route_scale = 2.5
norm_eps = 1e-06
MESH = pl.DeviceIdType.MESH
f32, bf16 = jnp.float32, jnp.bfloat16


def mm(a, b):
    return jnp.dot(a, b, preferred_element_type=f32)


def mm_nt(a, b):
    return lax.dot_general(a, b, (((1,), (1,)), ((), ())), preferred_element_type=f32)


def log2(n):
    assert n & (n - 1) == 0
    return n.bit_length() - 1


def iota2(shape, dim):
    return lax.broadcasted_iota(jnp.int32, shape, dim)


def onehot(target, shape):
    return jnp.where(iota2(shape, 1) == target, 1.0, 0.0).astype(bf16)


def layer_kernel(
    ep,
    tp,
    steps,
    heads,
    rp,
    lat,
    q_chunk,
    len_ref,
    hid_ref,
    gain_ref,
    chosen_ref,
    router_ref,
    q_hbm,
    kv_hbm,
    new_hbm,
    up_hbm,
    op_hbm,
    ein_hbm,
    eout_hbm,
    sin_hbm,
    sout_hbm,
    out_ref,
    q_v,
    kv_v,
    new_v,
    up_v,
    op_v,
    ein_v,
    eout_v,
    sin_v,
    sout_v,
    lat_send,
    lat_recv,
    vals_v,
    b_send,
    b_recv,
    t_send,
    t_recv,
    n_all,
    x_v,
    x_own,
    sh_v,
    f_send,
    f_recv,
    u_send,
    u_recv,
    ch_all,
    w_sem,
    ch_ss,
    ch_rs,
    a_ss,
    a_rs,
    b_ss,
    b_rs,
    t_ss,
    t_rs,
    c_ss,
    c_rs,
    d_ss,
    d_rs,
    f_ss,
    f_rs,
    u_ss,
    u_rs,
):
    my_ep, my_tp = lax.axis_index("ep"), lax.axis_index("tp")
    n = ep * tp
    me = my_ep * tp + my_tp
    pack = 16 // steps
    items = n * steps
    ep_items = tp * steps
    width = out_ref.shape[1]

    loads = [
        pltpu.make_async_copy(src, dst, w_sem.at[i])
        for i, (src, dst) in enumerate(
            [
                (q_hbm, q_v),
                (kv_hbm, kv_v),
                (new_hbm, new_v),
                (up_hbm, up_v),
                (op_hbm, op_v),
                (sin_hbm, sin_v),
                (sout_hbm, sout_v),
                (ein_hbm, ein_v),
                (eout_hbm, eout_v),
            ]
        )
    ]
    for load in loads:
        load.start()

    def dev(d):
        return {"ep": d // tp, "tp": d % tp}

    def ep_peer(o):
        return lax.rem(my_ep + o, ep)

    def tp_peer(o):
        return lax.rem(my_tp + o, tp)

    def remote(src, dst, ss, rs, where):
        return pltpu.make_async_remote_copy(
            src_ref=src, dst_ref=dst, send_sem=ss, recv_sem=rs, device_id=where, device_id_type=MESH
        )

    barrier = pltpu.get_barrier_semaphore()

    @pl.loop(1, n)
    def _(o):
        pl.semaphore_signal(
            barrier, inc=1, device_id=dev(lax.rem(me + o, n)), device_id_type=MESH
        )

    pl.semaphore_wait(barrier, n - 1)

    def chosen_copy(src, e):
        return remote(ch_all.at[my_ep], ch_all.at[src], ch_ss.at[e], ch_rs.at[src], {"ep": e})

    ch_all[my_ep] = chosen_ref[...]
    for o in range(1, ep):
        chosen_copy(my_ep, ep_peer(o)).start()

    def latent_copy(slot, d):
        return remote(lat_send.at[d], lat_recv.at[slot], a_ss.at[d], a_rs.at[slot], dev(d))

    for load in loads[:3]:
        load.wait()
    length = len_ref[0]
    dests = q_chunk // rp

    @pl.loop(0, n // dests)
    def _(c):
        q = q_v[pl.ds(c * dests, dests)].reshape(q_chunk, q_v.shape[2])
        kv = kv_v[...]
        new = new_v[...]
        cached = mm_nt(q, kv) * score_scale
        recent = mm_nt(q, new) * score_scale
        cached = jnp.where(iota2(cached.shape, 1) < length, cached, -1e30)
        row = iota2(recent.shape, 0) & (rp - 1)
        step = jnp.minimum(row >> log2(heads), steps - 1)
        recent = jnp.where(iota2(recent.shape, 1) <= step, recent, -1e30)
        highest = jnp.maximum(
            jnp.max(cached, axis=1, keepdims=True), jnp.max(recent, axis=1, keepdims=True)
        )
        cached = jnp.exp(cached - highest)
        recent = jnp.exp(recent - highest)
        total = jnp.sum(cached, axis=1, keepdims=True) + jnp.sum(recent, axis=1, keepdims=True)
        mixed = mm(cached.astype(bf16), kv[:, :lat]) + mm(recent.astype(bf16), new[:, :lat])
        lat_send[pl.ds(c * dests, dests)] = (mixed / total).astype(bf16).reshape(dests, rp, lat)

        @pl.loop(0, dests)
        def _(j):
            d = c * dests + j

            @pl.when(d != me)
            def _():
                latent_copy(me, d).start()

    lat_recv[me] = lat_send[me]
    loads[3].wait()
    loads[4].wait()

    @pl.loop(1, n)
    def _(o):
        d = lax.rem(me + o, n)
        latent_copy(d, d).wait_recv()

    shape = (heads * items, n * rp)
    r = iota2((shape[0], 1), 0)
    item = r & (items - 1)
    target = (
        (item >> log2(steps)) * rp + (item & (steps - 1)) * heads + (r >> log2(items))
    )
    by_head = mm(onehot(target, shape), lat_recv[...].reshape(n * rp, lat)).astype(bf16)
    vh = up_v.shape[2]
    for h in range(heads):
        vals_v[:, h * vh : (h + 1) * vh] = mm(
            by_head[h * items : (h + 1) * items], up_v[h]
        ).astype(bf16)

    def rs_copy(send, recv, ss, rs, k, slot, e):
        return remote(send.at[k, e], recv.at[k, slot], ss.at[k, e], rs.at[k, slot], {"ep": e})

    def tp_copy(send, recv, ss, rs, slot, t):
        return remote(send.at[t], recv.at[slot], ss.at[t], rs.at[slot], {"tp": t})

    def scatter_sum(part, extra, send, recv, ss, rs, send2, recv2, ss2, rs2):
        for k in range(pack):
            send[k] = part(k).astype(bf16).reshape(ep, ep_items, width)
            for o in range(1, ep):
                rs_copy(send, recv, ss, rs, k, my_ep, ep_peer(o)).start()
            recv[k, my_ep] = send[k, my_ep]
        sums = []
        for k in range(pack):
            for o in range(1, ep):
                rs_copy(send, recv, ss, rs, k, ep_peer(o), ep_peer(o)).wait_recv()
            total = jnp.sum(recv[k].astype(f32), axis=0)
            if extra is not None:
                total = total + extra(k)
            sums.append(total.astype(bf16))
        stacked = jnp.concatenate(sums, axis=0)
        r = iota2((tp * 16, 1), 0)
        target = (
            ((r & 15) >> log2(steps)) * ep_items + (r >> 4) * steps + (r & (steps - 1))
        )
        turned = mm(onehot(target, (tp * 16, pack * ep_items)), stacked).astype(bf16)
        send2[...] = turned.reshape(tp, 16, width)
        for o in range(1, tp):
            tp_copy(send2, recv2, ss2, rs2, my_tp, tp_peer(o)).start()
        recv2[my_tp] = send2[my_tp]
        for o in range(1, tp):
            tp_copy(send2, recv2, ss2, rs2, tp_peer(o), tp_peer(o)).wait_recv()
        return jnp.sum(recv2[...].astype(f32), axis=0)

    vals = vals_v[...]
    attention = scatter_sum(
        lambda k: mm(vals, op_v[:, k * width : (k + 1) * width]),
        None,
        b_send,
        b_recv,
        b_ss,
        b_rs,
        t_send,
        t_recv,
        t_ss,
        t_rs,
    )
    residual = hid_ref[...].astype(f32) + attention
    same = jnp.where(
        (iota2((16, 16), 0) & (steps - 1)) == (iota2((16, 16), 1) & (steps - 1)), 1.0, 0.0
    )
    squares = jnp.dot(
        same, residual * residual, precision=lax.Precision.HIGHEST, preferred_element_type=f32
    )
    mean_square = jnp.sum(squares, axis=1, keepdims=True) / (pack * width)
    normed = residual * lax.rsqrt(mean_square + norm_eps) * gain_ref[...].astype(f32)
    n_all[my_ep, my_tp] = normed.astype(bf16)

    def c_copy(slot, t):
        return remote(
            n_all.at[my_ep, my_tp], n_all.at[my_ep, slot], c_ss.at[t], c_rs.at[slot], {"tp": t}
        )

    def d_copy(t, slot, e):
        return remote(
            n_all.at[my_ep, t], n_all.at[slot, t], d_ss.at[t, e], d_rs.at[t, slot], {"ep": e}
        )

    for o in range(1, tp):
        c_copy(my_tp, tp_peer(o)).start()
    for o in range(1, ep):
        d_copy(my_tp, my_ep, ep_peer(o)).start()
    for p in range(1, tp):
        c_copy(tp_peer(p), tp_peer(p)).wait_recv()
        for o in range(1, ep):
            d_copy(tp_peer(p), my_ep, ep_peer(o)).start()

    def unpack(blocks, count, into):
        m = count * steps
        r = iota2((pack * m, 1), 0)
        item = r & (m - 1)
        target = (
            (item >> log2(steps)) * 16 + (r >> log2(m)) * steps + (item & (steps - 1))
        )
        flat = mm(onehot(target, (pack * m, count * 16)), blocks).astype(bf16)
        for k in range(pack):
            into[:, k * width : (k + 1) * width] = flat[k * m : (k + 1) * m]

    unpack(n_all[my_ep].reshape(tp * 16, width), tp, x_own)
    loads[5].wait()
    loads[6].wait()
    xo = x_own[...]
    shared_act = (jax.nn.silu(mm(xo, sin_v[0])) * mm(xo, sin_v[1])).astype(bf16)
    sh_v[...] = mm(shared_act, sout_v[...])
    loads[7].wait()
    loads[8].wait()
    for o in range(1, ep):
        chosen_copy(ep_peer(o), ep_peer(o)).wait_recv()
    for p in range(tp):
        for o in range(1, ep):
            d_copy(tp_peer(p), ep_peer(o), ep_peer(o)).wait_recv()

    unpack(n_all[...].reshape(n * 16, width), n, x_v)
    x = x_v[...]
    affinity = jax.nn.sigmoid(mm_nt(x, router_ref[...]))
    chosen = ch_all[...].reshape(items, ch_all.shape[2])[:, : affinity.shape[1]]
    scored = chosen * affinity
    mine = jnp.where(iota2(scored.shape, 1) == my_ep, scored, 0.0)
    gate = (
        route_scale
        * jnp.sum(mine, axis=1, keepdims=True)
        / jnp.sum(scored, axis=1, keepdims=True)
    )
    act = (jax.nn.silu(mm(x, ein_v[0])) * mm(x, ein_v[1])).astype(bf16)
    expert_sum = scatter_sum(
        lambda k: mm(act, eout_v[:, k * width : (k + 1) * width]) * gate,
        lambda k: sh_v[:, k * width : (k + 1) * width],
        f_send,
        f_recv,
        f_ss,
        f_rs,
        u_send,
        u_recv,
        u_ss,
        u_rs,
    )
    out_ref[...] = (residual + expert_sum).astype(bf16)

    @pl.loop(1, n)
    def _(o):
        d = lax.rem(me + o, n)
        latent_copy(me, d).wait_send()

    for o in range(1, ep):
        e = ep_peer(o)
        chosen_copy(my_ep, e).wait_send()
        for k in range(pack):
            rs_copy(b_send, b_recv, b_ss, b_rs, k, my_ep, e).wait_send()
            rs_copy(f_send, f_recv, f_ss, f_rs, k, my_ep, e).wait_send()
        for p in range(tp):
            d_copy(tp_peer(p), my_ep, e).wait_send()
    for o in range(1, tp):
        t = tp_peer(o)
        tp_copy(t_send, t_recv, t_ss, t_rs, my_tp, t).wait_send()
        tp_copy(u_send, u_recv, u_ss, u_rs, my_tp, t).wait_send()
        c_copy(my_tp, t).wait_send()


def on_device(
    ep,
    tp,
    hidden_in,
    queries,
    kv_cache,
    new_kv,
    lengths,
    expert_ids,
    value_up,
    out_proj,
    norm_gain,
    router,
    expert_in,
    expert_out,
    shared_in,
    shared_out,
):
    n = ep * tp
    rows, steps, d = hidden_in.shape
    heads, lat, vh = value_up.shape
    kvw = queries.shape[3]
    ctx = kv_cache.shape[1]
    assert rows == 1 and 16 % steps == 0
    pack = 16 // steps
    width = d // pack
    ep_items = tp * steps
    items = n * steps
    experts = router.shape[1]
    assert experts == ep
    rp = -(-steps * heads // 16) * 16
    q = queries[0].reshape(steps, n, heads, kvw).transpose(1, 0, 2, 3).reshape(n, steps * heads, kvw)
    q = jnp.pad(q, ((0, 0), (0, rp - steps * heads), (0, 0)))
    new = jnp.pad(new_kv[0], ((0, -steps % 16), (0, 0)))
    hid = hidden_in[0].reshape(steps, pack, width).transpose(1, 0, 2).reshape(16, width)
    gain = jnp.repeat(norm_gain.reshape(pack, width), steps, axis=0)
    e_pad = -(-experts // 16) * 16
    router_t = jnp.pad(router.T, ((0, e_pad - experts), (0, 0)))
    picked = expert_ids.reshape(ep_items, expert_ids.shape[2])
    lanes = lax.broadcasted_iota(jnp.int32, (1, 1, 128), 2)
    chosen = jnp.sum((picked[:, :, None] == lanes).astype(f32), axis=1)
    q_chunk = min(256, n * rp)
    hf = expert_in.shape[3]
    sf = shared_in.shape[2]

    vm, dma = pltpu.VMEM, pltpu.SemaphoreType.DMA
    scratch = [
        vm((n, rp, kvw), bf16),
        vm((ctx, kvw), bf16),
        vm(new.shape, bf16),
        vm(value_up.shape, bf16),
        vm((heads * vh, d), bf16),
        vm((2, d, hf), bf16),
        vm((hf, d), bf16),
        vm((2, d, sf), bf16),
        vm((sf, d), bf16),
        vm((n, rp, lat), bf16),
        vm((n, rp, lat), bf16),
        vm((items, heads * vh), bf16),
        vm((pack, ep, ep_items, width), bf16),
        vm((pack, ep, ep_items, width), bf16),
        vm((tp, 16, width), bf16),
        vm((tp, 16, width), bf16),
        vm((ep, tp, 16, width), bf16),
        vm((items, d), bf16),
        vm((ep_items, d), bf16),
        vm((ep_items, d), f32),
        vm((pack, ep, ep_items, width), bf16),
        vm((pack, ep, ep_items, width), bf16),
        vm((tp, 16, width), bf16),
        vm((tp, 16, width), bf16),
        vm((ep, ep_items, 128), f32),
        dma((9,)),
        dma((ep,)),
        dma((ep,)),
        dma((n,)),
        dma((n,)),
        dma((pack, ep)),
        dma((pack, ep)),
        dma((tp,)),
        dma((tp,)),
        dma((tp,)),
        dma((tp,)),
        dma((tp, ep)),
        dma((tp, ep)),
        dma((pack, ep)),
        dma((pack, ep)),
        dma((tp,)),
        dma((tp,)),
    ]
    vmem = pl.BlockSpec(memory_space=pltpu.VMEM)
    hbm = pl.BlockSpec(memory_space=pl.ANY)
    out = pl.pallas_call(
        functools.partial(layer_kernel, ep, tp, steps, heads, rp, lat, q_chunk),
        out_shape=jax.ShapeDtypeStruct((16, width), bf16),
        in_specs=[pl.BlockSpec(memory_space=pltpu.SMEM)] + [vmem] * 4 + [hbm] * 9,
        out_specs=vmem,
        scratch_shapes=scratch,
        compiler_params=pltpu.CompilerParams(
            collective_id=0, has_side_effects=True, vmem_limit_bytes=60 * 2**20
        ),
        name="layer",
    )(
        lengths,
        hid,
        gain,
        chosen,
        router_t,
        q,
        kv_cache[0],
        new,
        value_up,
        out_proj.reshape(heads * vh, d),
        expert_in[0],
        expert_out[0],
        shared_in,
        shared_out,
    )
    return out.reshape(pack, steps, width).transpose(1, 0, 2).reshape(1, steps, d)


def solution(mesh):
    rows = ("groups", "ep", "tp")
    in_specs = (
        P(rows, None, None),
        P(rows, None, None, None),
        P(rows, None, None),
        P(rows, None, None),
        P(rows),
        P(("groups", "ep"), None, None),
        P(("ep", "tp"), None, None),
        P(("ep", "tp"), None, None),
        P(),
        P(),
        P("ep", None, None, "tp"),
        P("ep", "tp", None),
        P(None, None, "tp"),
        P("tp", None),
    )
    body = functools.partial(on_device, mesh.shape["ep"], mesh.shape["tp"])
    return jax.shard_map(
        body, mesh=mesh, in_specs=in_specs, out_specs=P(rows, None, None), check_vma=False
    )
```

```python
import functools

import jax
import jax.numpy as jnp
from jax import lax
from jax.experimental import pallas as pl
from jax.experimental.pallas import tpu as pltpu
from jax.sharding import PartitionSpec as P

score_scale = 192.0 ** (-0.5)
route_scale = 2.5
norm_eps = 1e-06
MESH = pl.DeviceIdType.MESH
f32, bf16 = jnp.float32, jnp.bfloat16


def mm(a, b):
    return jnp.dot(a, b, preferred_element_type=f32)


def mm_nt(a, b):
    return lax.dot_general(a, b, (((1,), (1,)), ((), ())), preferred_element_type=f32)


def log2(n):
    assert n & (n - 1) == 0
    return n.bit_length() - 1


def iota2(shape, dim):
    return lax.broadcasted_iota(jnp.int32, shape, dim)


def onehot(target, shape):
    return jnp.where(iota2(shape, 1) == target, 1.0, 0.0).astype(bf16)


def layer_kernel(
    ep,
    tp,
    steps,
    heads,
    rp,
    lat,
    q_chunk,
    len_ref,
    hid_ref,
    gain_ref,
    ids_ref,
    router_ref,
    new_v,
    q_hbm,
    kv_hbm,
    up_hbm,
    op_hbm,
    ein_hbm,
    eout_hbm,
    sin_hbm,
    sout_hbm,
    out_ref,
    q_v,
    kv_v,
    up_v,
    op_v,
    ein_v,
    eout_v,
    sin_v,
    sout_v,
    lat_send,
    lat_recv,
    vals_v,
    b_send,
    b_recv,
    t_send,
    t_recv,
    n_all,
    x_v,
    x_own,
    sh_v,
    f_send,
    f_recv,
    u_send,
    u_recv,
    ch_all,
    w_sem,
    ch_ss,
    ch_rs,
    a_ss,
    a_rs,
    b_ss,
    b_rs,
    t_ss,
    t_rs,
    c_ss,
    c_rs,
    d_ss,
    d_rs,
    f_ss,
    f_rs,
    u_ss,
    u_rs,
):
    my_ep, my_tp = lax.axis_index("ep"), lax.axis_index("tp")
    n = ep * tp
    me = my_ep * tp + my_tp
    pack = 16 // steps
    items = n * steps
    ep_items = tp * steps
    width = out_ref.shape[1] // pack

    loads = [
        pltpu.make_async_copy(src, dst, w_sem.at[i])
        for i, (src, dst) in enumerate(
            [
                (q_hbm, q_v),
                (kv_hbm, kv_v),
                (up_hbm, up_v),
                (op_hbm, op_v),
                (sin_hbm, sin_v),
                (sout_hbm, sout_v),
                (ein_hbm, ein_v),
                (eout_hbm, eout_v),
            ]
        )
    ]
    for load in loads:
        load.start()

    def dev(d):
        return {"ep": d // tp, "tp": d % tp}

    def ep_peer(o):
        return lax.rem(my_ep + o, ep)

    def tp_peer(o):
        return lax.rem(my_tp + o, tp)

    def remote(src, dst, ss, rs, where):
        return pltpu.make_async_remote_copy(
            src_ref=src, dst_ref=dst, send_sem=ss, recv_sem=rs, device_id=where, device_id_type=MESH
        )

    barrier = pltpu.get_barrier_semaphore()

    @pl.loop(1, n)
    def _(o):
        pl.semaphore_signal(
            barrier, inc=1, device_id=dev(lax.rem(me + o, n)), device_id_type=MESH
        )

    def chosen_copy(src, e):
        return remote(ch_all.at[my_ep], ch_all.at[src], ch_ss.at[e], ch_rs.at[src], {"ep": e})

    shape = (ep_items, ch_all.shape[2])
    row, lane = iota2(shape, 0), iota2(shape, 1)
    chosen = jnp.zeros(shape, f32)
    for i in range(ep_items):
        for k in range(ids_ref.shape[1]):
            hit = (row == i) & (lane == ids_ref[i // steps, k, i % steps])
            chosen = chosen + jnp.where(hit, 1.0, 0.0)
    ch_all[my_ep] = chosen

    def owner(o):
        return my_ep ^ lax.rem(o, ep), my_tp ^ (o // ep)

    def latent_copy(o):
        e, t = owner(o)
        return remote(
            lat_send.at[o], lat_recv.at[me], a_ss.at[o], a_rs.at[me], {"ep": e, "tp": t}
        )

    def latent_arrival(o):
        e, t = owner(o)
        d = e * tp + t
        return remote(
            lat_send.at[o], lat_recv.at[d], a_ss.at[o], a_rs.at[d], {"ep": e, "tp": t}
        )

    for load in loads[:2]:
        load.wait()
    length = len_ref[0]
    dests = q_chunk // rp
    chunks = n // dests

    def attend(c):
        first = (chunks - 1 - c) * dests
        row = iota2((q_chunk, 1), 0)
        o = first + (row >> log2(rp))
        within = row & (rp - 1)
        step = within >> log2(heads)
        e = my_ep ^ (o & (ep - 1))
        t = my_tp ^ (o >> log2(ep))
        head = (e * tp + t) * heads + (within & (heads - 1))
        q = jnp.zeros((q_chunk, kv_v.shape[0]), f32)
        for s in range(steps):
            pick = onehot(jnp.where(step == s, head, -1), (q_chunk, q_v.shape[2]))
            q = q + mm_nt(pick, q_v[s])
        q = q.astype(bf16)
        kv = kv_v[...]
        new = new_v[...]
        cached = mm(q, kv) * score_scale
        recent = mm_nt(q, new) * score_scale
        cached = jnp.where(iota2(cached.shape, 1) < length, cached, -1e30)
        step = jnp.minimum(step, steps - 1)
        recent = jnp.where(iota2(recent.shape, 1) <= step, recent, -1e30)
        highest = jnp.maximum(
            jnp.max(cached, axis=1, keepdims=True), jnp.max(recent, axis=1, keepdims=True)
        )
        cached = jnp.exp(cached - highest)
        recent = jnp.exp(recent - highest)
        total = jnp.sum(cached, axis=1, keepdims=True) + jnp.sum(recent, axis=1, keepdims=True)
        mixed = mm_nt(cached.astype(bf16), kv[:lat])
        mixed = mixed + mm(recent.astype(bf16), new[:, :lat])
        mixed = (mixed / total).astype(bf16).reshape(dests, rp, lat)
        lat_send[pl.ds(first, dests)] = mixed

    def send_block(c):
        @pl.loop(0, dests)
        def _(j):
            o = (chunks - c) * dests - 1 - j

            @pl.when(o > 0)
            def _():
                latent_copy(o).start()

    attend(0)
    pl.semaphore_wait(barrier, n - 1)
    send_block(0)
    for o in range(1, ep):
        chosen_copy(my_ep, ep_peer(o)).start()

    @pl.loop(1, chunks)
    def _(c):
        attend(c)
        send_block(c)

    lat_recv[me] = lat_send[0]
    loads[2].wait()
    loads[3].wait()

    @pl.loop(1, n)
    def _(o):
        latent_arrival(o).wait_recv()

    shape = (heads * items, n * rp)
    r = iota2((shape[0], 1), 0)
    item = r & (items - 1)
    target = (
        (item >> log2(steps)) * rp + (item & (steps - 1)) * heads + (r >> log2(items))
    )
    by_head = mm(onehot(target, shape), lat_recv[...].reshape(n * rp, lat)).astype(bf16)
    vh = up_v.shape[2]
    for h in range(heads):
        vals_v[:, h * vh : (h + 1) * vh] = mm(
            by_head[h * items : (h + 1) * items], up_v[h]
        ).astype(bf16)

    def rs_copy(send, recv, ss, rs, k, slot, e):
        return remote(send.at[k, e], recv.at[k, slot], ss.at[k, e], rs.at[k, slot], {"ep": e})

    def tp_copy(send, recv, ss, rs, slot, t):
        return remote(send.at[t], recv.at[slot], ss.at[t], rs.at[slot], {"tp": t})

    def scatter_sum(part, extra, send, recv, ss, rs, send2, recv2, ss2, rs2):
        for k in range(pack):
            send[k] = part(k).astype(bf16).reshape(ep, ep_items, width)
            for o in range(1, ep):
                rs_copy(send, recv, ss, rs, k, my_ep, ep_peer(o)).start()
            recv[k, my_ep] = send[k, my_ep]
        sums = []
        for k in range(pack):
            for o in range(1, ep):
                rs_copy(send, recv, ss, rs, k, ep_peer(o), ep_peer(o)).wait_recv()
            total = jnp.sum(recv[k].astype(f32), axis=0)
            if extra is not None:
                total = total + extra(k)
            sums.append(total.astype(bf16))
        stacked = jnp.concatenate(sums, axis=0)
        r = iota2((tp * 16, 1), 0)
        target = (
            ((r & 15) >> log2(steps)) * ep_items + (r >> 4) * steps + (r & (steps - 1))
        )
        turned = mm(onehot(target, (tp * 16, pack * ep_items)), stacked).astype(bf16)
        send2[...] = turned.reshape(tp, 16, width)
        for o in range(1, tp):
            tp_copy(send2, recv2, ss2, rs2, my_tp, tp_peer(o)).start()
        recv2[my_tp] = send2[my_tp]
        for o in range(1, tp):
            tp_copy(send2, recv2, ss2, rs2, tp_peer(o), tp_peer(o)).wait_recv()
        return jnp.sum(recv2[...].astype(f32), axis=0)

    vals = vals_v[...]
    attention = scatter_sum(
        lambda k: mm(vals, op_v[:, k * width : (k + 1) * width]),
        None,
        b_send,
        b_recv,
        b_ss,
        b_rs,
        t_send,
        t_recv,
        t_ss,
        t_rs,
    )
    hidden = hid_ref[...].astype(f32)
    gain = gain_ref[...].astype(f32).reshape(1, pack * width)

    def columns(a, k):
        return a[:, k * width : (k + 1) * width]

    residual = attention + jnp.concatenate([columns(hidden, k) for k in range(pack)], axis=0)
    gain = jnp.concatenate(
        [jnp.broadcast_to(columns(gain, k), (steps, width)) for k in range(pack)], axis=0
    )
    same = jnp.where(
        (iota2((16, 16), 0) & (steps - 1)) == (iota2((16, 16), 1) & (steps - 1)), 1.0, 0.0
    )
    squares = jnp.dot(
        same, residual * residual, precision=lax.Precision.HIGHEST, preferred_element_type=f32
    )
    mean_square = jnp.sum(squares, axis=1, keepdims=True) / (pack * width)
    normed = residual * lax.rsqrt(mean_square + norm_eps) * gain
    n_all[my_ep, my_tp] = normed.astype(bf16)

    def c_copy(slot, t):
        return remote(
            n_all.at[my_ep, my_tp], n_all.at[my_ep, slot], c_ss.at[t], c_rs.at[slot], {"tp": t}
        )

    def d_copy(t, slot, e):
        return remote(
            n_all.at[my_ep, t], n_all.at[slot, t], d_ss.at[t, e], d_rs.at[t, slot], {"ep": e}
        )

    for o in range(1, tp):
        c_copy(my_tp, tp_peer(o)).start()
    for o in range(1, ep):
        d_copy(my_tp, my_ep, ep_peer(o)).start()
    for p in range(1, tp):
        c_copy(tp_peer(p), tp_peer(p)).wait_recv()
        for o in range(1, ep):
            d_copy(tp_peer(p), my_ep, ep_peer(o)).start()

    def unpack(blocks, count, into):
        m = count * steps
        r = iota2((pack * m, 1), 0)
        item = r & (m - 1)
        target = (
            (item >> log2(steps)) * 16 + (r >> log2(m)) * steps + (item & (steps - 1))
        )
        flat = mm(onehot(target, (pack * m, count * 16)), blocks).astype(bf16)
        for k in range(pack):
            into[:, k * width : (k + 1) * width] = flat[k * m : (k + 1) * m]

    unpack(n_all[my_ep].reshape(tp * 16, width), tp, x_own)
    loads[4].wait()
    loads[5].wait()
    xo = x_own[...]
    shared_act = (jax.nn.silu(mm(xo, sin_v[0])) * mm(xo, sin_v[1])).astype(bf16)
    sh_v[...] = mm(shared_act, sout_v[...])
    loads[6].wait()
    loads[7].wait()
    for o in range(1, ep):
        chosen_copy(ep_peer(o), ep_peer(o)).wait_recv()
    for p in range(tp):
        for o in range(1, ep):
            d_copy(tp_peer(p), ep_peer(o), ep_peer(o)).wait_recv()

    unpack(n_all[...].reshape(n * 16, width), n, x_v)
    x = x_v[...]
    affinity = jax.nn.sigmoid(mm_nt(x, router_ref[...]))
    chosen = ch_all[...].reshape(items, ch_all.shape[2])[:, : affinity.shape[1]]
    scored = chosen * affinity
    mine = jnp.where(iota2(scored.shape, 1) == my_ep, scored, 0.0)
    gate = (
        route_scale
        * jnp.sum(mine, axis=1, keepdims=True)
        / jnp.sum(scored, axis=1, keepdims=True)
    )
    act = (jax.nn.silu(mm(x, ein_v[0])) * mm(x, ein_v[1])).astype(bf16)
    expert_sum = scatter_sum(
        lambda k: mm(act, eout_v[:, k * width : (k + 1) * width]) * gate,
        lambda k: sh_v[:, k * width : (k + 1) * width],
        f_send,
        f_recv,
        f_ss,
        f_rs,
        u_send,
        u_recv,
        u_ss,
        u_rs,
    )
    result = residual + expert_sum
    for k in range(pack):
        out_ref[:, k * width : (k + 1) * width] = result[k * steps : (k + 1) * steps].astype(bf16)

    @pl.loop(1, n)
    def _(o):
        latent_copy(o).wait_send()

    for o in range(1, ep):
        e = ep_peer(o)
        chosen_copy(my_ep, e).wait_send()
        for k in range(pack):
            rs_copy(b_send, b_recv, b_ss, b_rs, k, my_ep, e).wait_send()
            rs_copy(f_send, f_recv, f_ss, f_rs, k, my_ep, e).wait_send()
        for p in range(tp):
            d_copy(tp_peer(p), my_ep, e).wait_send()
    for o in range(1, tp):
        t = tp_peer(o)
        tp_copy(t_send, t_recv, t_ss, t_rs, my_tp, t).wait_send()
        tp_copy(u_send, u_recv, u_ss, u_rs, my_tp, t).wait_send()
        c_copy(my_tp, t).wait_send()


def on_device(
    ep,
    tp,
    hidden_in,
    queries,
    kv_cache,
    new_kv,
    lengths,
    expert_ids,
    value_up,
    out_proj,
    norm_gain,
    router,
    expert_in,
    expert_out,
    shared_in,
    shared_out,
):
    n = ep * tp
    rows, steps, d = hidden_in.shape
    heads, lat, vh = value_up.shape
    kvw = queries.shape[3]
    ctx = kv_cache.shape[1]
    assert rows == 1 and 16 % steps == 0
    pack = 16 // steps
    width = d // pack
    ep_items = tp * steps
    items = n * steps
    experts = router.shape[1]
    assert experts == ep
    rp = -(-steps * heads // 16) * 16
    q_chunk = min(256, n * rp)
    hf = expert_in.shape[3]
    sf = shared_in.shape[2]

    vm, dma = pltpu.VMEM, pltpu.SemaphoreType.DMA
    scratch = [
        vm((steps, kvw, n * heads), bf16),
        vm((kvw, ctx), bf16),
        vm(value_up.shape, bf16),
        vm((heads * vh, d), bf16),
        vm((2, d, hf), bf16),
        vm((hf, d), bf16),
        vm((2, d, sf), bf16),
        vm((sf, d), bf16),
        vm((n, rp, lat), bf16),
        vm((n, rp, lat), bf16),
        vm((items, heads * vh), bf16),
        vm((pack, ep, ep_items, width), bf16),
        vm((pack, ep, ep_items, width), bf16),
        vm((tp, 16, width), bf16),
        vm((tp, 16, width), bf16),
        vm((ep, tp, 16, width), bf16),
        vm((items, d), bf16),
        vm((ep_items, d), bf16),
        vm((ep_items, d), f32),
        vm((pack, ep, ep_items, width), bf16),
        vm((pack, ep, ep_items, width), bf16),
        vm((tp, 16, width), bf16),
        vm((tp, 16, width), bf16),
        vm((ep, ep_items, 128), f32),
        dma((8,)),
        dma((ep,)),
        dma((ep,)),
        dma((n,)),
        dma((n,)),
        dma((pack, ep)),
        dma((pack, ep)),
        dma((tp,)),
        dma((tp,)),
        dma((tp,)),
        dma((tp,)),
        dma((tp, ep)),
        dma((tp, ep)),
        dma((pack, ep)),
        dma((pack, ep)),
        dma((tp,)),
        dma((tp,)),
    ]
    vmem = pl.BlockSpec(memory_space=pltpu.VMEM)
    hbm = pl.BlockSpec(memory_space=pl.ANY)
    smem = pl.BlockSpec(memory_space=pltpu.SMEM)
    out = pl.pallas_call(
        functools.partial(layer_kernel, ep, tp, steps, heads, rp, lat, q_chunk),
        out_shape=jax.ShapeDtypeStruct((steps, d), bf16),
        in_specs=[smem, vmem, vmem, smem, vmem, vmem] + [hbm] * 8,
        out_specs=vmem,
        scratch_shapes=scratch,
        compiler_params=pltpu.CompilerParams(
            collective_id=0, has_side_effects=True, vmem_limit_bytes=60 * 2**20
        ),
        name="layer",
    )(
        lengths,
        hidden_in[0],
        norm_gain,
        expert_ids.transpose(0, 2, 1),
        router.T,
        new_kv[0],
        queries[0].transpose(0, 2, 1),
        kv_cache[0].T,
        value_up,
        out_proj.reshape(heads * vh, d),
        expert_in[0],
        expert_out[0],
        shared_in,
        shared_out,
    )
    return out[None]


def solution(mesh):
    rows = ("groups", "ep", "tp")
    in_specs = (
        P(rows, None, None),
        P(rows, None, None, None),
        P(rows, None, None),
        P(rows, None, None),
        P(rows),
        P(("groups", "ep"), None, None),
        P(("ep", "tp"), None, None),
        P(("ep", "tp"), None, None),
        P(),
        P(),
        P("ep", None, None, "tp"),
        P("ep", "tp", None),
        P(None, None, "tp"),
        P("tp", None),
    )
    body = functools.partial(on_device, mesh.shape["ep"], mesh.shape["tp"])
    return jax.shard_map(
        body, mesh=mesh, in_specs=in_specs, out_specs=P(rows, None, None), check_vma=False
    )
```

```python
import functools

import jax
import jax.numpy as jnp
from jax import lax
from jax.experimental import pallas as pl
from jax.experimental.pallas import tpu as pltpu
from jax.sharding import PartitionSpec as P

score_scale = 192.0 ** (-0.5)
route_scale = 2.5
norm_eps = 1e-06
MESH = pl.DeviceIdType.MESH
f32, bf16 = jnp.float32, jnp.bfloat16


def mm(a, b):
    return jnp.dot(a, b, preferred_element_type=f32)


def mm_nt(a, b):
    return lax.dot_general(a, b, (((1,), (1,)), ((), ())), preferred_element_type=f32)


def log2(n):
    assert n & (n - 1) == 0
    return n.bit_length() - 1


def iota2(shape, dim):
    return lax.broadcasted_iota(jnp.int32, shape, dim)


def onehot(target, shape):
    return jnp.where(iota2(shape, 1) == target, 1.0, 0.0).astype(bf16)


def layer_kernel(
    ep,
    tp,
    steps,
    heads,
    rp,
    lat,
    q_chunk,
    len_ref,
    hid_ref,
    gain_ref,
    ids_ref,
    router_ref,
    new_v,
    q_hbm,
    kv_hbm,
    up_hbm,
    op_hbm,
    ein_hbm,
    eout_hbm,
    sin_hbm,
    sout_hbm,
    out_ref,
    q_v,
    kv_v,
    up_v,
    op_v,
    ein_v,
    eout_v,
    sin_v,
    sout_v,
    lat_send,
    lat_recv,
    vals_v,
    b_split,
    b_pair,
    b_send,
    b_recv,
    t_send,
    t_recv,
    n_all,
    x_v,
    x_own,
    sh_v,
    f_split,
    f_pair,
    f_send,
    f_recv,
    u_send,
    u_recv,
    ch_all,
    w_sem,
    ch_ss,
    ch_rs,
    a_ss,
    a_rs,
    b_pss,
    b_prs,
    b_ss,
    b_rs,
    t_ss,
    t_rs,
    c_ss,
    c_rs,
    d_ss,
    d_rs,
    g_ss,
    g_rs,
    f_pss,
    f_prs,
    f_ss,
    f_rs,
    u_ss,
    u_rs,
):
    my_ep, my_tp = lax.axis_index("ep"), lax.axis_index("tp")
    n = ep * tp
    me = my_ep * tp + my_tp
    pack = 16 // steps
    items = n * steps
    ep_items = tp * steps
    width = out_ref.shape[1] // pack

    loads = [
        pltpu.make_async_copy(src, dst, w_sem.at[i])
        for i, (src, dst) in enumerate(
            [
                (q_hbm, q_v),
                (kv_hbm, kv_v),
                (up_hbm, up_v),
                (op_hbm, op_v),
                (sin_hbm, sin_v),
                (sout_hbm, sout_v),
                (ein_hbm, ein_v),
                (eout_hbm, eout_v),
            ]
        )
    ]
    for load in loads:
        load.start()

    def dev(d):
        return {"ep": d // tp, "tp": d % tp}

    def ep_peer(o):
        return lax.rem(my_ep + o, ep)

    def tp_peer(o):
        return lax.rem(my_tp + o, tp)

    def remote(src, dst, ss, rs, where):
        return pltpu.make_async_remote_copy(
            src_ref=src, dst_ref=dst, send_sem=ss, recv_sem=rs, device_id=where, device_id_type=MESH
        )

    barrier = pltpu.get_barrier_semaphore()

    @pl.loop(1, n)
    def _(o):
        pl.semaphore_signal(
            barrier, inc=1, device_id=dev(lax.rem(me + o, n)), device_id_type=MESH
        )

    def chosen_copy(src, e):
        return remote(ch_all.at[my_ep], ch_all.at[src], ch_ss.at[e], ch_rs.at[src], {"ep": e})

    shape = (ep_items, ch_all.shape[2])
    row, lane = iota2(shape, 0), iota2(shape, 1)
    chosen = jnp.zeros(shape, f32)
    for i in range(ep_items):
        for k in range(ids_ref.shape[1]):
            hit = (row == i) & (lane == ids_ref[i // steps, k, i % steps])
            chosen = chosen + jnp.where(hit, 1.0, 0.0)
    ch_all[my_ep] = chosen

    def owner(o):
        return my_ep ^ lax.rem(o, ep), my_tp ^ (o // ep)

    def latent_copy(o):
        e, t = owner(o)
        return remote(
            lat_send.at[o], lat_recv.at[me], a_ss.at[o], a_rs.at[me], {"ep": e, "tp": t}
        )

    def latent_arrival(o):
        e, t = owner(o)
        d = e * tp + t
        return remote(
            lat_send.at[o], lat_recv.at[d], a_ss.at[o], a_rs.at[d], {"ep": e, "tp": t}
        )

    for load in loads[:2]:
        load.wait()
    length = len_ref[0]
    dests = q_chunk // rp
    chunks = n // dests

    def attend(c):
        first = (chunks - 1 - c) * dests
        row = iota2((q_chunk, 1), 0)
        o = first + (row >> log2(rp))
        within = row & (rp - 1)
        step = within >> log2(heads)
        e = my_ep ^ (o & (ep - 1))
        t = my_tp ^ (o >> log2(ep))
        head = (e * tp + t) * heads + (within & (heads - 1))
        q = jnp.zeros((q_chunk, kv_v.shape[0]), f32)
        for s in range(steps):
            pick = onehot(jnp.where(step == s, head, -1), (q_chunk, q_v.shape[2]))
            q = q + mm_nt(pick, q_v[s])
        q = q.astype(bf16)
        kv = kv_v[...]
        new = new_v[...]
        cached = mm(q, kv) * score_scale
        recent = mm_nt(q, new) * score_scale
        cached = jnp.where(iota2(cached.shape, 1) < length, cached, -1e30)
        step = jnp.minimum(step, steps - 1)
        recent = jnp.where(iota2(recent.shape, 1) <= step, recent, -1e30)
        highest = jnp.maximum(
            jnp.max(cached, axis=1, keepdims=True), jnp.max(recent, axis=1, keepdims=True)
        )
        cached = jnp.exp(cached - highest)
        recent = jnp.exp(recent - highest)
        total = jnp.sum(cached, axis=1, keepdims=True) + jnp.sum(recent, axis=1, keepdims=True)
        mixed = mm_nt(cached.astype(bf16), kv[:lat])
        mixed = mixed + mm(recent.astype(bf16), new[:, :lat])
        mixed = (mixed / total).astype(bf16).reshape(dests, rp, lat)
        lat_send[pl.ds(first, dests)] = mixed

    def send_block(c):
        @pl.loop(0, dests)
        def _(j):
            o = (chunks - c) * dests - 1 - j

            @pl.when(o > 0)
            def _():
                latent_copy(o).start()

    attend(0)
    pl.semaphore_wait(barrier, n - 1)
    send_block(0)
    for o in range(1, ep):
        chosen_copy(my_ep, ep_peer(o)).start()

    @pl.loop(1, chunks)
    def _(c):
        attend(c)
        send_block(c)

    lat_recv[me] = lat_send[0]
    loads[2].wait()
    loads[3].wait()

    @pl.loop(1, n)
    def _(o):
        latent_arrival(o).wait_recv()

    shape = (heads * items, n * rp)
    r = iota2((shape[0], 1), 0)
    item = r & (items - 1)
    target = (
        (item >> log2(steps)) * rp + (item & (steps - 1)) * heads + (r >> log2(items))
    )
    by_head = mm(onehot(target, shape), lat_recv[...].reshape(n * rp, lat)).astype(bf16)
    vh = up_v.shape[2]
    for h in range(heads):
        vals_v[:, h * vh : (h + 1) * vh] = mm(
            by_head[h * items : (h + 1) * items], up_v[h]
        ).astype(bf16)

    chips = ep // 2
    my_chip, my_core = my_ep // 2, lax.rem(my_ep, 2)
    other = {"ep": my_chip * 2 + 1 - my_core}

    def chip_peer(o):
        return lax.rem(my_chip + o, chips)

    def core_copy(send, pair, ss, rs, k):
        return remote(send.at[k, 1 - my_core], pair.at[k], ss.at[k], rs.at[k], other)

    def rs_copy(send, recv, ss, rs, k, slot, c):
        return remote(
            send.at[k, c], recv.at[k, slot], ss.at[k, c], rs.at[k, slot], {"ep": c * 2 + my_core}
        )

    def tp_copy(send, recv, ss, rs, slot, t):
        return remote(send.at[t], recv.at[slot], ss.at[t], rs.at[slot], {"tp": t})

    def scatter_sum(part, extra, pairs, chips_bufs, pair_sems, chip_sems, send2, recv2, ss2, rs2):
        split, pair = pairs
        send, recv = chips_bufs
        for k in range(pack + 1):
            if k < pack:
                block = part(k).astype(bf16).reshape(chips, 2, ep_items, width)
                split[k, 0] = block[:, 0]
                split[k, 1] = block[:, 1]
                core_copy(split, pair, *pair_sems, k).start()
            if k > 0:
                j = k - 1
                core_copy(split, pair, *pair_sems, j).wait_recv()
                send[j] = (split[j, my_core].astype(f32) + pair[j].astype(f32)).astype(bf16)
                for o in range(1, chips):
                    rs_copy(send, recv, *chip_sems, j, my_chip, chip_peer(o)).start()
                recv[j, my_chip] = send[j, my_chip]
        sums = []
        for k in range(pack):
            for o in range(1, chips):
                c = chip_peer(o)
                rs_copy(send, recv, *chip_sems, k, c, c).wait_recv()
            total = jnp.sum(recv[k].astype(f32), axis=0)
            if extra is not None:
                total = total + extra(k)
            sums.append(total.astype(bf16))
        stacked = jnp.concatenate(sums, axis=0)
        r = iota2((tp * 16, 1), 0)
        target = (
            ((r & 15) >> log2(steps)) * ep_items + (r >> 4) * steps + (r & (steps - 1))
        )
        turned = mm(onehot(target, (tp * 16, pack * ep_items)), stacked).astype(bf16)
        send2[...] = turned.reshape(tp, 16, width)
        for o in range(1, tp):
            tp_copy(send2, recv2, ss2, rs2, my_tp, tp_peer(o)).start()
        recv2[my_tp] = send2[my_tp]
        for o in range(1, tp):
            tp_copy(send2, recv2, ss2, rs2, tp_peer(o), tp_peer(o)).wait_recv()
        return jnp.sum(recv2[...].astype(f32), axis=0)

    vals = vals_v[...]
    attention = scatter_sum(
        lambda k: mm(vals, op_v[:, k * width : (k + 1) * width]),
        None,
        (b_split, b_pair),
        (b_send, b_recv),
        (b_pss, b_prs),
        (b_ss, b_rs),
        t_send,
        t_recv,
        t_ss,
        t_rs,
    )
    hidden = hid_ref[...].astype(f32)
    gain = gain_ref[...].astype(f32).reshape(1, pack * width)

    def columns(a, k):
        return a[:, k * width : (k + 1) * width]

    residual = attention + jnp.concatenate([columns(hidden, k) for k in range(pack)], axis=0)
    gain = jnp.concatenate(
        [jnp.broadcast_to(columns(gain, k), (steps, width)) for k in range(pack)], axis=0
    )
    same = jnp.where(
        (iota2((16, 16), 0) & (steps - 1)) == (iota2((16, 16), 1) & (steps - 1)), 1.0, 0.0
    )
    squares = jnp.dot(
        same, residual * residual, precision=lax.Precision.HIGHEST, preferred_element_type=f32
    )
    mean_square = jnp.sum(squares, axis=1, keepdims=True) / (pack * width)
    normed = residual * lax.rsqrt(mean_square + norm_eps) * gain
    n_all[my_ep, my_tp] = normed.astype(bf16)

    def c_copy(slot, t):
        return remote(
            n_all.at[my_ep, my_tp], n_all.at[my_ep, slot], c_ss.at[t], c_rs.at[slot], {"tp": t}
        )

    def d_copy(t, slot, c):
        return remote(
            n_all.at[my_ep, t],
            n_all.at[slot * 2 + my_core, t],
            d_ss.at[t, c],
            d_rs.at[t, slot],
            {"ep": c * 2 + my_core},
        )

    def g_copy(t, c):
        block = n_all.at[c * 2 + my_core, t]
        return remote(block, block, g_ss.at[t, c], g_rs.at[t, c], other)

    def g_arrival(t, c):
        block = n_all.at[c * 2 + 1 - my_core, t]
        return remote(block, block, g_ss.at[t, c], g_rs.at[t, c], other)

    def pass_on(t):
        for o in range(1, chips):
            d_copy(t, my_chip, chip_peer(o)).start()
        g_copy(t, my_chip).start()

    for o in range(1, tp):
        c_copy(my_tp, tp_peer(o)).start()
    pass_on(my_tp)
    for p in range(1, tp):
        c_copy(tp_peer(p), tp_peer(p)).wait_recv()
        pass_on(tp_peer(p))

    def unpack(blocks, count, into):
        m = count * steps
        r = iota2((pack * m, 1), 0)
        item = r & (m - 1)
        target = (
            (item >> log2(steps)) * 16 + (r >> log2(m)) * steps + (item & (steps - 1))
        )
        flat = mm(onehot(target, (pack * m, count * 16)), blocks).astype(bf16)
        for k in range(pack):
            into[:, k * width : (k + 1) * width] = flat[k * m : (k + 1) * m]

    unpack(n_all[my_ep].reshape(tp * 16, width), tp, x_own)
    loads[4].wait()
    loads[5].wait()
    xo = x_own[...]
    shared_act = (jax.nn.silu(mm(xo, sin_v[0])) * mm(xo, sin_v[1])).astype(bf16)
    sh_v[...] = mm(shared_act, sout_v[...])
    loads[6].wait()
    loads[7].wait()
    for o in range(1, ep):
        chosen_copy(ep_peer(o), ep_peer(o)).wait_recv()
    for p in range(tp):
        for o in range(1, chips):
            d_copy(tp_peer(p), chip_peer(o), chip_peer(o)).wait_recv()
            g_copy(tp_peer(p), chip_peer(o)).start()
    for p in range(tp):
        for o in range(chips):
            g_arrival(tp_peer(p), chip_peer(o)).wait_recv()

    unpack(n_all[...].reshape(n * 16, width), n, x_v)
    x = x_v[...]
    affinity = jax.nn.sigmoid(mm_nt(x, router_ref[...]))
    chosen = ch_all[...].reshape(items, ch_all.shape[2])[:, : affinity.shape[1]]
    scored = chosen * affinity
    mine = jnp.where(iota2(scored.shape, 1) == my_ep, scored, 0.0)
    gate = (
        route_scale
        * jnp.sum(mine, axis=1, keepdims=True)
        / jnp.sum(scored, axis=1, keepdims=True)
    )
    act = (jax.nn.silu(mm(x, ein_v[0])) * mm(x, ein_v[1])).astype(bf16)
    expert_sum = scatter_sum(
        lambda k: mm(act, eout_v[:, k * width : (k + 1) * width]) * gate,
        lambda k: sh_v[:, k * width : (k + 1) * width],
        (f_split, f_pair),
        (f_send, f_recv),
        (f_pss, f_prs),
        (f_ss, f_rs),
        u_send,
        u_recv,
        u_ss,
        u_rs,
    )
    result = residual + expert_sum
    for k in range(pack):
        out_ref[:, k * width : (k + 1) * width] = result[k * steps : (k + 1) * steps].astype(bf16)

    @pl.loop(1, n)
    def _(o):
        latent_copy(o).wait_send()

    for o in range(1, ep):
        e = ep_peer(o)
        chosen_copy(my_ep, e).wait_send()
    for k in range(pack):
        core_copy(b_split, b_pair, b_pss, b_prs, k).wait_send()
        core_copy(f_split, f_pair, f_pss, f_prs, k).wait_send()
    for o in range(1, chips):
        c = chip_peer(o)
        for k in range(pack):
            rs_copy(b_send, b_recv, b_ss, b_rs, k, my_chip, c).wait_send()
            rs_copy(f_send, f_recv, f_ss, f_rs, k, my_chip, c).wait_send()
        for p in range(tp):
            d_copy(tp_peer(p), my_chip, c).wait_send()
    for p in range(tp):
        for o in range(chips):
            g_copy(tp_peer(p), chip_peer(o)).wait_send()
    for o in range(1, tp):
        t = tp_peer(o)
        tp_copy(t_send, t_recv, t_ss, t_rs, my_tp, t).wait_send()
        tp_copy(u_send, u_recv, u_ss, u_rs, my_tp, t).wait_send()
        c_copy(my_tp, t).wait_send()


def on_device(
    ep,
    tp,
    hidden_in,
    queries,
    kv_cache,
    new_kv,
    lengths,
    expert_ids,
    value_up,
    out_proj,
    norm_gain,
    router,
    expert_in,
    expert_out,
    shared_in,
    shared_out,
):
    n = ep * tp
    rows, steps, d = hidden_in.shape
    heads, lat, vh = value_up.shape
    kvw = queries.shape[3]
    ctx = kv_cache.shape[1]
    assert rows == 1 and 16 % steps == 0 and ep % 2 == 0
    pack = 16 // steps
    width = d // pack
    ep_items = tp * steps
    items = n * steps
    experts = router.shape[1]
    assert experts == ep
    rp = -(-steps * heads // 16) * 16
    q_chunk = min(256, n * rp)
    hf = expert_in.shape[3]
    sf = shared_in.shape[2]

    vm, dma = pltpu.VMEM, pltpu.SemaphoreType.DMA
    scratch = [
        vm((steps, kvw, n * heads), bf16),
        vm((kvw, ctx), bf16),
        vm(value_up.shape, bf16),
        vm((heads * vh, d), bf16),
        vm((2, d, hf), bf16),
        vm((hf, d), bf16),
        vm((2, d, sf), bf16),
        vm((sf, d), bf16),
        vm((n, rp, lat), bf16),
        vm((n, rp, lat), bf16),
        vm((items, heads * vh), bf16),
        vm((pack, 2, ep // 2, ep_items, width), bf16),
        vm((pack, ep // 2, ep_items, width), bf16),
        vm((pack, ep // 2, ep_items, width), bf16),
        vm((pack, ep // 2, ep_items, width), bf16),
        vm((tp, 16, width), bf16),
        vm((tp, 16, width), bf16),
        vm((ep, tp, 16, width), bf16),
        vm((items, d), bf16),
        vm((ep_items, d), bf16),
        vm((ep_items, d), f32),
        vm((pack, 2, ep // 2, ep_items, width), bf16),
        vm((pack, ep // 2, ep_items, width), bf16),
        vm((pack, ep // 2, ep_items, width), bf16),
        vm((pack, ep // 2, ep_items, width), bf16),
        vm((tp, 16, width), bf16),
        vm((tp, 16, width), bf16),
        vm((ep, ep_items, 128), f32),
        dma((8,)),
        dma((ep,)),
        dma((ep,)),
        dma((n,)),
        dma((n,)),
        dma((pack,)),
        dma((pack,)),
        dma((pack, ep // 2)),
        dma((pack, ep // 2)),
        dma((tp,)),
        dma((tp,)),
        dma((tp,)),
        dma((tp,)),
        dma((tp, ep // 2)),
        dma((tp, ep // 2)),
        dma((tp, ep // 2)),
        dma((tp, ep // 2)),
        dma((pack,)),
        dma((pack,)),
        dma((pack, ep // 2)),
        dma((pack, ep // 2)),
        dma((tp,)),
        dma((tp,)),
    ]
    vmem = pl.BlockSpec(memory_space=pltpu.VMEM)
    hbm = pl.BlockSpec(memory_space=pl.ANY)
    smem = pl.BlockSpec(memory_space=pltpu.SMEM)
    out = pl.pallas_call(
        functools.partial(layer_kernel, ep, tp, steps, heads, rp, lat, q_chunk),
        out_shape=jax.ShapeDtypeStruct((steps, d), bf16),
        in_specs=[smem, vmem, vmem, smem, vmem, vmem] + [hbm] * 8,
        out_specs=vmem,
        scratch_shapes=scratch,
        compiler_params=pltpu.CompilerParams(
            collective_id=0, has_side_effects=True, vmem_limit_bytes=60 * 2**20
        ),
        name="layer",
    )(
        lengths,
        hidden_in[0],
        norm_gain,
        expert_ids.transpose(0, 2, 1),
        router.T,
        new_kv[0],
        queries[0].transpose(0, 2, 1),
        kv_cache[0].T,
        value_up,
        out_proj.reshape(heads * vh, d),
        expert_in[0],
        expert_out[0],
        shared_in,
        shared_out,
    )
    return out[None]


def solution(mesh):
    rows = ("groups", "ep", "tp")
    in_specs = (
        P(rows, None, None),
        P(rows, None, None, None),
        P(rows, None, None),
        P(rows, None, None),
        P(rows),
        P(("groups", "ep"), None, None),
        P(("ep", "tp"), None, None),
        P(("ep", "tp"), None, None),
        P(),
        P(),
        P("ep", None, None, "tp"),
        P("ep", "tp", None),
        P(None, None, "tp"),
        P("tp", None),
    )
    body = functools.partial(on_device, mesh.shape["ep"], mesh.shape["tp"])
    return jax.shard_map(
        body, mesh=mesh, in_specs=in_specs, out_specs=P(rows, None, None), check_vma=False
    )
```

```python
import functools

import jax
import jax.numpy as jnp
from jax import lax
from jax.experimental import pallas as pl
from jax.experimental.pallas import tpu as pltpu
from jax.sharding import PartitionSpec as P

score_scale = 192.0 ** (-0.5)
route_scale = 2.5
norm_eps = 1e-06
MESH = pl.DeviceIdType.MESH
f32, bf16 = jnp.float32, jnp.bfloat16


def mm(a, b):
    return jnp.dot(a, b, preferred_element_type=f32)


def mm_nt(a, b):
    return lax.dot_general(a, b, (((1,), (1,)), ((), ())), preferred_element_type=f32)


def log2(n):
    assert n & (n - 1) == 0
    return n.bit_length() - 1


def iota2(shape, dim):
    return lax.broadcasted_iota(jnp.int32, shape, dim)


def onehot(target, shape):
    return jnp.where(iota2(shape, 1) == target, 1.0, 0.0).astype(bf16)


def layer_kernel(
    ep,
    tp,
    steps,
    heads,
    rp,
    lat,
    q_chunk,
    len_ref,
    hid_ref,
    gain_ref,
    ids_ref,
    router_ref,
    new_v,
    q_hbm,
    kv_hbm,
    up_hbm,
    op_hbm,
    ein_hbm,
    eout_hbm,
    sin_hbm,
    sout_hbm,
    out_ref,
    q_v,
    kv_v,
    up_v,
    op_v,
    ein_v,
    eout_v,
    sin_v,
    sout_v,
    lat_send,
    lat_recv,
    vals_v,
    b_split,
    b_pair,
    b_send,
    b_recv,
    t_send,
    t_recv,
    n_all,
    x_v,
    x_own,
    sh_v,
    f_split,
    f_pair,
    f_send,
    f_recv,
    u_send,
    u_recv,
    ch_all,
    w_sem,
    ch_ss,
    ch_rs,
    a_ss,
    a_rs,
    b_pss,
    b_prs,
    b_ss,
    b_rs,
    t_ss,
    t_rs,
    c_ss,
    c_rs,
    d_ss,
    d_rs,
    g_ss,
    g_rs,
    f_pss,
    f_prs,
    f_ss,
    f_rs,
    u_ss,
    u_rs,
):
    my_ep, my_tp = lax.axis_index("ep"), lax.axis_index("tp")
    n = ep * tp
    me = my_ep * tp + my_tp
    pack = 16 // steps
    items = n * steps
    ep_items = tp * steps
    width = out_ref.shape[1] // pack

    loads = [
        pltpu.make_async_copy(src, dst, w_sem.at[i])
        for i, (src, dst) in enumerate(
            [
                (q_hbm, q_v),
                (kv_hbm, kv_v),
                (up_hbm, up_v),
                (op_hbm, op_v),
                (sin_hbm, sin_v),
                (sout_hbm, sout_v),
                (ein_hbm, ein_v),
                (eout_hbm, eout_v),
            ]
        )
    ]
    for load in loads[:2]:
        load.start()

    def dev(d):
        return {"ep": d // tp, "tp": d % tp}

    def ep_peer(o):
        return lax.rem(my_ep + o, ep)

    def tp_peer(o):
        return lax.rem(my_tp + o, tp)

    def remote(src, dst, ss, rs, where):
        return pltpu.make_async_remote_copy(
            src_ref=src, dst_ref=dst, send_sem=ss, recv_sem=rs, device_id=where, device_id_type=MESH
        )

    barrier = pltpu.get_barrier_semaphore()

    @pl.loop(1, n)
    def _(o):
        pl.semaphore_signal(
            barrier, inc=1, device_id=dev(lax.rem(me + o, n)), device_id_type=MESH
        )

    def chosen_copy(src, e):
        return remote(ch_all.at[my_ep], ch_all.at[src], ch_ss.at[e], ch_rs.at[src], {"ep": e})

    shape = (ep_items, ch_all.shape[2])
    row, lane = iota2(shape, 0), iota2(shape, 1)
    chosen = jnp.zeros(shape, f32)
    for i in range(ep_items):
        for k in range(ids_ref.shape[1]):
            hit = (row == i) & (lane == ids_ref[i // steps, k, i % steps])
            chosen = chosen + jnp.where(hit, 1.0, 0.0)
    ch_all[my_ep] = chosen

    def owner(o):
        return my_ep ^ lax.rem(o, ep), my_tp ^ (o // ep)

    def latent_copy(o):
        e, t = owner(o)
        return remote(
            lat_send.at[o], lat_recv.at[me], a_ss.at[o], a_rs.at[me], {"ep": e, "tp": t}
        )

    def latent_arrival(o):
        e, t = owner(o)
        d = e * tp + t
        return remote(
            lat_send.at[o], lat_recv.at[d], a_ss.at[o], a_rs.at[d], {"ep": e, "tp": t}
        )

    for load in loads[:2]:
        load.wait()
    for load in loads[2:]:
        load.start()
    length = len_ref[0]
    dests = q_chunk // rp
    chunks = n // dests

    def attend(c):
        first = (chunks - 1 - c) * dests
        row = iota2((q_chunk, 1), 0)
        o = first + (row >> log2(rp))
        within = row & (rp - 1)
        step = within >> log2(heads)
        e = my_ep ^ (o & (ep - 1))
        t = my_tp ^ (o >> log2(ep))
        head = (e * tp + t) * heads + (within & (heads - 1))
        q = jnp.zeros((q_chunk, kv_v.shape[0]), f32)
        for s in range(steps):
            pick = onehot(jnp.where(step == s, head, -1), (q_chunk, q_v.shape[2]))
            q = q + mm_nt(pick, q_v[s])
        q = q.astype(bf16)
        kv = kv_v[...]
        new = new_v[...]
        cached = mm(q, kv) * score_scale
        recent = mm_nt(q, new) * score_scale
        cached = jnp.where(iota2(cached.shape, 1) < length, cached, -1e30)
        step = jnp.minimum(step, steps - 1)
        recent = jnp.where(iota2(recent.shape, 1) <= step, recent, -1e30)
        highest = jnp.maximum(
            jnp.max(cached, axis=1, keepdims=True), jnp.max(recent, axis=1, keepdims=True)
        )
        cached = jnp.exp(cached - highest)
        recent = jnp.exp(recent - highest)
        total = jnp.sum(cached, axis=1, keepdims=True) + jnp.sum(recent, axis=1, keepdims=True)
        mixed = mm_nt(cached.astype(bf16), kv[:lat])
        mixed = mixed + mm(recent.astype(bf16), new[:, :lat])
        mixed = (mixed / total).astype(bf16).reshape(dests, rp, lat)
        lat_send[pl.ds(first, dests)] = mixed

    def send_block(c):
        @pl.loop(0, dests)
        def _(j):
            o = (chunks - c) * dests - 1 - j

            @pl.when(o > 0)
            def _():
                latent_copy(o).start()

    attend(0)
    pl.semaphore_wait(barrier, n - 1)
    send_block(0)
    for o in range(1, ep):
        chosen_copy(my_ep, ep_peer(o)).start()

    @pl.loop(1, chunks)
    def _(c):
        attend(c)
        send_block(c)

    lat_recv[me] = lat_send[0]
    loads[2].wait()
    loads[3].wait()

    @pl.loop(1, n)
    def _(o):
        latent_arrival(o).wait_recv()

    shape = (heads * items, n * rp)
    r = iota2((shape[0], 1), 0)
    item = r & (items - 1)
    target = (
        (item >> log2(steps)) * rp + (item & (steps - 1)) * heads + (r >> log2(items))
    )
    by_head = mm(onehot(target, shape), lat_recv[...].reshape(n * rp, lat)).astype(bf16)
    vh = up_v.shape[2]
    for h in range(heads):
        vals_v[:, h * vh : (h + 1) * vh] = mm(
            by_head[h * items : (h + 1) * items], up_v[h]
        ).astype(bf16)

    chips = ep // 2
    my_chip, my_core = my_ep // 2, lax.rem(my_ep, 2)
    other = {"ep": my_chip * 2 + 1 - my_core}

    def chip_peer(o):
        return lax.rem(my_chip + o, chips)

    def core_copy(send, pair, ss, rs, k):
        return remote(send.at[k, 1 - my_core], pair.at[k], ss.at[k], rs.at[k], other)

    def rs_copy(send, recv, ss, rs, k, slot, c):
        return remote(
            send.at[k, c], recv.at[k, slot], ss.at[k, c], rs.at[k, slot], {"ep": c * 2 + my_core}
        )

    def tp_copy(send, recv, ss, rs, slot, t):
        return remote(send.at[t], recv.at[slot], ss.at[t], rs.at[slot], {"tp": t})

    def scatter_sum(part, extra, pairs, chips_bufs, pair_sems, chip_sems, send2, recv2, ss2, rs2):
        split, pair = pairs
        send, recv = chips_bufs
        for k in range(pack + 1):
            if k < pack:
                block = part(k).astype(bf16).reshape(chips, 2, ep_items, width)
                split[k, 0] = block[:, 0]
                split[k, 1] = block[:, 1]
                core_copy(split, pair, *pair_sems, k).start()
            if k > 0:
                j = k - 1
                core_copy(split, pair, *pair_sems, j).wait_recv()
                send[j] = (split[j, my_core].astype(f32) + pair[j].astype(f32)).astype(bf16)
                for o in range(1, chips):
                    rs_copy(send, recv, *chip_sems, j, my_chip, chip_peer(o)).start()
                recv[j, my_chip] = send[j, my_chip]
        sums = []
        for k in range(pack):
            for o in range(1, chips):
                c = chip_peer(o)
                rs_copy(send, recv, *chip_sems, k, c, c).wait_recv()
            total = jnp.sum(recv[k].astype(f32), axis=0)
            if extra is not None:
                total = total + extra(k)
            sums.append(total.astype(bf16))
        stacked = jnp.concatenate(sums, axis=0)
        r = iota2((tp * 16, 1), 0)
        target = (
            ((r & 15) >> log2(steps)) * ep_items + (r >> 4) * steps + (r & (steps - 1))
        )
        turned = mm(onehot(target, (tp * 16, pack * ep_items)), stacked).astype(bf16)
        send2[...] = turned.reshape(tp, 16, width)
        for o in range(1, tp):
            tp_copy(send2, recv2, ss2, rs2, my_tp, tp_peer(o)).start()
        recv2[my_tp] = send2[my_tp]
        for o in range(1, tp):
            tp_copy(send2, recv2, ss2, rs2, tp_peer(o), tp_peer(o)).wait_recv()
        return jnp.sum(recv2[...].astype(f32), axis=0)

    vals = vals_v[...]
    attention = scatter_sum(
        lambda k: mm(vals, op_v[:, k * width : (k + 1) * width]),
        None,
        (b_split, b_pair),
        (b_send, b_recv),
        (b_pss, b_prs),
        (b_ss, b_rs),
        t_send,
        t_recv,
        t_ss,
        t_rs,
    )
    hidden = hid_ref[...].astype(f32)
    gain = gain_ref[...].astype(f32).reshape(1, pack * width)

    def columns(a, k):
        return a[:, k * width : (k + 1) * width]

    residual = attention + jnp.concatenate([columns(hidden, k) for k in range(pack)], axis=0)
    gain = jnp.concatenate(
        [jnp.broadcast_to(columns(gain, k), (steps, width)) for k in range(pack)], axis=0
    )
    same = jnp.where(
        (iota2((16, 16), 0) & (steps - 1)) == (iota2((16, 16), 1) & (steps - 1)), 1.0, 0.0
    )
    squares = jnp.dot(
        same, residual * residual, precision=lax.Precision.HIGHEST, preferred_element_type=f32
    )
    mean_square = jnp.sum(squares, axis=1, keepdims=True) / (pack * width)
    normed = residual * lax.rsqrt(mean_square + norm_eps) * gain
    n_all[my_ep, my_tp] = normed.astype(bf16)

    def c_copy(slot, t):
        return remote(
            n_all.at[my_ep, my_tp], n_all.at[my_ep, slot], c_ss.at[t], c_rs.at[slot], {"tp": t}
        )

    def d_copy(t, slot, c):
        return remote(
            n_all.at[my_ep, t],
            n_all.at[slot * 2 + my_core, t],
            d_ss.at[t, c],
            d_rs.at[t, slot],
            {"ep": c * 2 + my_core},
        )

    def g_copy(t, c):
        block = n_all.at[c * 2 + my_core, t]
        return remote(block, block, g_ss.at[t, c], g_rs.at[t, c], other)

    def g_arrival(t, c):
        block = n_all.at[c * 2 + 1 - my_core, t]
        return remote(block, block, g_ss.at[t, c], g_rs.at[t, c], other)

    def pass_on(t):
        for o in range(1, chips):
            d_copy(t, my_chip, chip_peer(o)).start()
        g_copy(t, my_chip).start()

    for o in range(1, tp):
        c_copy(my_tp, tp_peer(o)).start()
    pass_on(my_tp)
    for p in range(1, tp):
        c_copy(tp_peer(p), tp_peer(p)).wait_recv()
        pass_on(tp_peer(p))

    def unpack(blocks, count, into):
        m = count * steps
        r = iota2((pack * m, 1), 0)
        item = r & (m - 1)
        target = (
            (item >> log2(steps)) * 16 + (r >> log2(m)) * steps + (item & (steps - 1))
        )
        flat = mm(onehot(target, (pack * m, count * 16)), blocks).astype(bf16)
        for k in range(pack):
            into[:, k * width : (k + 1) * width] = flat[k * m : (k + 1) * m]

    unpack(n_all[my_ep].reshape(tp * 16, width), tp, x_own)
    loads[4].wait()
    loads[5].wait()
    xo = x_own[...]
    shared_act = (jax.nn.silu(mm(xo, sin_v[0])) * mm(xo, sin_v[1])).astype(bf16)
    sh_v[...] = mm(shared_act, sout_v[...])
    loads[6].wait()
    loads[7].wait()
    for o in range(1, ep):
        chosen_copy(ep_peer(o), ep_peer(o)).wait_recv()
    for p in range(tp):
        for o in range(1, chips):
            d_copy(tp_peer(p), chip_peer(o), chip_peer(o)).wait_recv()
            g_copy(tp_peer(p), chip_peer(o)).start()
    for p in range(tp):
        for o in range(chips):
            g_arrival(tp_peer(p), chip_peer(o)).wait_recv()

    unpack(n_all[...].reshape(n * 16, width), n, x_v)
    x = x_v[...]
    affinity = jax.nn.sigmoid(mm_nt(x, router_ref[...]))
    chosen = ch_all[...].reshape(items, ch_all.shape[2])[:, : affinity.shape[1]]
    scored = chosen * affinity
    mine = jnp.where(iota2(scored.shape, 1) == my_ep, scored, 0.0)
    gate = (
        route_scale
        * jnp.sum(mine, axis=1, keepdims=True)
        / jnp.sum(scored, axis=1, keepdims=True)
    )
    act = (jax.nn.silu(mm(x, ein_v[0])) * mm(x, ein_v[1])).astype(bf16)
    expert_sum = scatter_sum(
        lambda k: mm(act, eout_v[:, k * width : (k + 1) * width]) * gate,
        lambda k: sh_v[:, k * width : (k + 1) * width],
        (f_split, f_pair),
        (f_send, f_recv),
        (f_pss, f_prs),
        (f_ss, f_rs),
        u_send,
        u_recv,
        u_ss,
        u_rs,
    )
    result = residual + expert_sum
    for k in range(pack):
        out_ref[:, k * width : (k + 1) * width] = result[k * steps : (k + 1) * steps].astype(bf16)

    @pl.loop(1, n)
    def _(o):
        latent_copy(o).wait_send()

    for o in range(1, ep):
        e = ep_peer(o)
        chosen_copy(my_ep, e).wait_send()
    for k in range(pack):
        core_copy(b_split, b_pair, b_pss, b_prs, k).wait_send()
        core_copy(f_split, f_pair, f_pss, f_prs, k).wait_send()
    for o in range(1, chips):
        c = chip_peer(o)
        for k in range(pack):
            rs_copy(b_send, b_recv, b_ss, b_rs, k, my_chip, c).wait_send()
            rs_copy(f_send, f_recv, f_ss, f_rs, k, my_chip, c).wait_send()
        for p in range(tp):
            d_copy(tp_peer(p), my_chip, c).wait_send()
    for p in range(tp):
        for o in range(chips):
            g_copy(tp_peer(p), chip_peer(o)).wait_send()
    for o in range(1, tp):
        t = tp_peer(o)
        tp_copy(t_send, t_recv, t_ss, t_rs, my_tp, t).wait_send()
        tp_copy(u_send, u_recv, u_ss, u_rs, my_tp, t).wait_send()
        c_copy(my_tp, t).wait_send()


def on_device(
    ep,
    tp,
    hidden_in,
    queries,
    kv_cache,
    new_kv,
    lengths,
    expert_ids,
    value_up,
    out_proj,
    norm_gain,
    router,
    expert_in,
    expert_out,
    shared_in,
    shared_out,
):
    n = ep * tp
    rows, steps, d = hidden_in.shape
    heads, lat, vh = value_up.shape
    kvw = queries.shape[3]
    ctx = kv_cache.shape[1]
    assert rows == 1 and 16 % steps == 0 and ep % 2 == 0
    pack = 16 // steps
    width = d // pack
    ep_items = tp * steps
    items = n * steps
    experts = router.shape[1]
    assert experts == ep
    rp = -(-steps * heads // 16) * 16
    q_chunk = min(256, n * rp)
    hf = expert_in.shape[3]
    sf = shared_in.shape[2]

    vm, dma = pltpu.VMEM, pltpu.SemaphoreType.DMA
    scratch = [
        vm((steps, kvw, n * heads), bf16),
        vm((kvw, ctx), bf16),
        vm(value_up.shape, bf16),
        vm((heads * vh, d), bf16),
        vm((2, d, hf), bf16),
        vm((hf, d), bf16),
        vm((2, d, sf), bf16),
        vm((sf, d), bf16),
        vm((n, rp, lat), bf16),
        vm((n, rp, lat), bf16),
        vm((items, heads * vh), bf16),
        vm((pack, 2, ep // 2, ep_items, width), bf16),
        vm((pack, ep // 2, ep_items, width), bf16),
        vm((pack, ep // 2, ep_items, width), bf16),
        vm((pack, ep // 2, ep_items, width), bf16),
        vm((tp, 16, width), bf16),
        vm((tp, 16, width), bf16),
        vm((ep, tp, 16, width), bf16),
        vm((items, d), bf16),
        vm((ep_items, d), bf16),
        vm((ep_items, d), f32),
        vm((pack, 2, ep // 2, ep_items, width), bf16),
        vm((pack, ep // 2, ep_items, width), bf16),
        vm((pack, ep // 2, ep_items, width), bf16),
        vm((pack, ep // 2, ep_items, width), bf16),
        vm((tp, 16, width), bf16),
        vm((tp, 16, width), bf16),
        vm((ep, ep_items, 128), f32),
        dma((8,)),
        dma((ep,)),
        dma((ep,)),
        dma((n,)),
        dma((n,)),
        dma((pack,)),
        dma((pack,)),
        dma((pack, ep // 2)),
        dma((pack, ep // 2)),
        dma((tp,)),
        dma((tp,)),
        dma((tp,)),
        dma((tp,)),
        dma((tp, ep // 2)),
        dma((tp, ep // 2)),
        dma((tp, ep // 2)),
        dma((tp, ep // 2)),
        dma((pack,)),
        dma((pack,)),
        dma((pack, ep // 2)),
        dma((pack, ep // 2)),
        dma((tp,)),
        dma((tp,)),
    ]
    vmem = pl.BlockSpec(memory_space=pltpu.VMEM)
    hbm = pl.BlockSpec(memory_space=pl.ANY)
    smem = pl.BlockSpec(memory_space=pltpu.SMEM)
    out = pl.pallas_call(
        functools.partial(layer_kernel, ep, tp, steps, heads, rp, lat, q_chunk),
        out_shape=jax.ShapeDtypeStruct((steps, d), bf16),
        in_specs=[smem, vmem, vmem, smem, vmem, vmem] + [hbm] * 8,
        out_specs=vmem,
        scratch_shapes=scratch,
        compiler_params=pltpu.CompilerParams(
            collective_id=0, has_side_effects=True, vmem_limit_bytes=60 * 2**20
        ),
        name="layer",
    )(
        lengths,
        hidden_in[0],
        norm_gain,
        expert_ids.transpose(0, 2, 1),
        router.T,
        new_kv[0],
        queries[0].transpose(0, 2, 1),
        kv_cache[0].T,
        value_up,
        out_proj.reshape(heads * vh, d),
        expert_in[0],
        expert_out[0],
        shared_in,
        shared_out,
    )
    return out[None]


def solution(mesh):
    rows = ("groups", "ep", "tp")
    in_specs = (
        P(rows, None, None),
        P(rows, None, None, None),
        P(rows, None, None),
        P(rows, None, None),
        P(rows),
        P(("groups", "ep"), None, None),
        P(("ep", "tp"), None, None),
        P(("ep", "tp"), None, None),
        P(),
        P(),
        P("ep", None, None, "tp"),
        P("ep", "tp", None),
        P(None, None, "tp"),
        P("tp", None),
    )
    body = functools.partial(on_device, mesh.shape["ep"], mesh.shape["tp"])
    return jax.shard_map(
        body, mesh=mesh, in_specs=in_specs, out_specs=P(rows, None, None), check_vma=False
    )
```
